256 devices in a mesh: seq: 32 (over y, z), head: 4 (over x_hi, core), rep: 2 (over x_lo).
Axes of the slice: x: 4 (x_hi: 2, x_lo: 2; x = x_hi * 2 + x_lo), y: 4, z: 8, core: 2. Of those that a mesh axis runs over, the one named last changes fastest.
Arguments:
- queries: bfloat16 [32768, 512], P(('rep', 'seq'), 'head'), parts along dimension 0, may hold values from -6 to 6
- keys: bfloat16 [32768, 512], P(('rep', 'seq'), 'head'), parts along dimension 0, may hold values from -6 to 6
- values: bfloat16 [32768, 512], P(('rep', 'seq'), 'head'), parts along dimension 0, may hold values from -6 to 6
- out_grad: bfloat16 [32768, 512], P(('rep', 'seq'), 'head'), parts along dimension 0, may hold values from -6 to 6
- block_mask: int32 [128, 128], replicated, may hold values 0 or 1
- block_order: int32 [128], replicated, may hold values from 0 to 127, each once
Outputs:
- query_grad: float32 [32768, 512], P(('rep', 'seq'), 'head'), parts along dimension 0
- key_grad: float32 [32768, 512], P(('rep', 'seq'), 'head'), parts along dimension 0
- value_grad: float32 [32768, 512], P(('rep', 'seq'), 'head'), parts along dimension 0
The draws below stay inside these ranges and needn't reach their ends.
There are 2 independent parts, one for each index of `rep`. The reference program is written for one: setup_inputs(seed, part) draws one part's arguments, and reference() takes and returns one part's arrays. A program takes and returns all parts, laid end to end along the dimension named above; an argument that names none is the same for every part. Nothing has to cross between parts.
Inputs may be any that keep to these rules, and one draw needn't show every extreme that they name: `block_order`: a permutation of the 128 blocks.
All inputs are finite; a program needn't handle non-finite values.
Results may differ from the reference program's by a relative error of at most 0.0029.
Values may be sent and summed in bfloat16 or wider, within the bound.
No kernel may reach another device: no remote copies, remote signals or barrier semaphores. Data moves between devices by JAX's collectives and lax.ppermute only.
A program may use at most 64 MiB of HBM per device.

```python
import jax
import jax.numpy as jnp
from jax import lax

DH = 128
HEADS = 4
D = 512
BLK = 128
TOK_DEV = 512
TOKENS = 16384
NB = 128


def set_ends(array, stream_key, least, largest):
    longest = array.shape.index(max(array.shape))
    spots = []
    for shift in (0, 1):
        where = [jax.random.randint(jax.random.fold_in(stream_key, axis), (), 0, length) for axis, length in enumerate(array.shape)]
        where[longest] = (where[longest] + shift) % array.shape[longest]
        spots.append(tuple(where))
    return array.at[spots[0]].set(least).at[spots[1]].set(largest)


def steps_of(key, extent, split, smallest, largest):
    gain, own = 1.0, jax.random.fold_in(key, 6)
    for dim, blocks in split:
        steps = jnp.exp(jax.random.uniform(jax.random.fold_in(own, dim), (blocks,), jnp.float32, smallest / len(split), largest / len(split)))
        gain = gain * jnp.repeat(steps, extent[dim] // blocks).reshape([-1 if axis == dim else 1 for axis in range(len(extent))])
    return gain


def gaussian(stream_key, dims, width, limit, cuts=(), held_as=jnp.bfloat16):
    values = jax.random.normal(stream_key, dims, jnp.float32) * width
    if len(cuts) > 0:
        values = steps_of(stream_key, dims, cuts, -0.22, 0.18) * values
    return jnp.clip(values, min=-limit, max=limit).astype(held_as)


def setup_inputs(seed: int = 0, part: int = 0) -> dict:
    key_of = jax.random.split(jax.random.key(seed), 7)
    part_splits = jax.random.split(jax.random.fold_in(key_of[6], part), 7)
    queries = gaussian(part_splits[0], (TOKENS, D), 1.0, 6.0, ((0, 32), (1, 4)))
    keys = gaussian(part_splits[1], (TOKENS, D), 1.0, 6.0, ((0, 32), (1, 4)))
    values = gaussian(part_splits[2], (TOKENS, D), 1.0, 6.0, ((0, 32), (1, 4)))
    out_grad = gaussian(part_splits[3], (TOKENS, D), 1.0, 6.0, ((0, 32), (1, 4)))
    block_mask = set_ends((jax.random.randint(key_of[4], (NB, NB), 0, 10) < 1).astype(jnp.int32), jax.random.fold_in(key_of[4], 1), 0, 1)
    block_order = jax.random.permutation(key_of[5], NB).astype(jnp.int32)
    return {"queries": queries, "keys": keys, "values": values, "out_grad": out_grad, "block_mask": block_mask, "block_order": block_order}


def row_rates(block_mask, orig_block, pos):
    ids = jnp.arange(NB, dtype=jnp.int32)
    below = lax.optimization_barrier(jnp.sum(block_mask * (ids[None, :] < ids[:, None]).astype(jnp.int32), axis=1))
    diag = lax.optimization_barrier(jnp.sum(block_mask * (ids[None, :] == ids[:, None]).astype(jnp.int32), axis=1))
    count = BLK * below[orig_block] + diag[orig_block] * (pos % BLK + 1)
    return 1.0 / jnp.sqrt(jnp.maximum(count, 1).astype(jnp.float32))

def reference(queries, keys, values, out_grad, block_mask, block_order):
    rows = jnp.arange(TOKENS, dtype=jnp.int32)
    orig_block = block_order[rows // BLK].astype(jnp.int32)
    pos = orig_block * BLK + rows % BLK
    rates = row_rates(block_mask, orig_block, pos)
    scale = DH ** (-0.5)
    qf = queries.astype(jnp.float32).reshape(TOKENS, HEADS, DH)
    kf = keys.astype(jnp.float32).reshape(TOKENS, HEADS, DH)
    vf = values.astype(jnp.float32).reshape(TOKENS, HEADS, DH)
    gf = out_grad.astype(jnp.float32).reshape(TOKENS, HEADS, DH)
    nblocks = TOKENS // TOK_DEV

    def one_block(carry, index):
        key_acc, value_acc = carry
        start = (index * TOK_DEV).astype(jnp.int32)
        q_blk = lax.dynamic_slice_in_dim(qf, start, TOK_DEV, 0)
        g_blk = lax.dynamic_slice_in_dim(gf, start, TOK_DEV, 0)
        pos_q = lax.dynamic_slice_in_dim(pos, start, TOK_DEV, 0)
        ob_q = lax.dynamic_slice_in_dim(orig_block, start, TOK_DEV, 0)
        rate_q = lax.dynamic_slice_in_dim(rates, start, TOK_DEV, 0)
        live = (block_mask[ob_q][:, orig_block] > 0) & (pos[None, :] <= pos_q[:, None])
        scores = jnp.einsum('qhd,khd->hqk', q_blk, kf) * scale
        sig = jax.nn.sigmoid(scores)
        weights = jnp.where(live[None], scores * sig * rate_q[None, :, None], 0.0)
        weights = lax.optimization_barrier(weights.astype(jnp.bfloat16)).astype(jnp.float32)
        d_weights = jnp.einsum('qhd,khd->hqk', g_blk, vf)
        d_scores = jnp.where(live[None], d_weights * rate_q[None, :, None] * (sig * (1.0 + scores * (1.0 - sig))), 0.0)
        d_scores = lax.optimization_barrier(d_scores.astype(jnp.bfloat16)).astype(jnp.float32)
        q_grad = jnp.einsum('hqk,khd->qhd', d_scores, kf) * scale
        key_acc = key_acc + jnp.einsum('hqk,qhd->khd', d_scores, q_blk) * scale
        value_acc = value_acc + jnp.einsum('hqk,qhd->khd', weights, g_blk)
        return ((key_acc, value_acc), q_grad)
    zeros = jnp.zeros((TOKENS, HEADS, DH), jnp.float32)
    (key_acc, value_acc), q_parts = lax.scan(one_block, (zeros, zeros), jnp.arange(nblocks, dtype=jnp.int32))
    query_grad = q_parts.reshape(TOKENS, HEADS * DH)
    return (query_grad, key_acc.reshape(TOKENS, HEADS * DH), value_acc.reshape(TOKENS, HEADS * DH))
```

```python
import functools

import jax
import jax.numpy as jnp
from jax import lax
from jax.experimental import pallas as pl
from jax.experimental.pallas import tpu as pltpu
from jax.sharding import PartitionSpec as P

BLK = 128
NZ = 8
NY = 4
OWN = 4
NK = NY * OWN
UNROLL = 4
SPARE = 8
GROUPS = ((0, 1, 2, 3, 4, 5, 6, 7),)
bf16, f32, i32 = jnp.bfloat16, jnp.float32, jnp.int32


def list_sizes():
    return [len(g) * OWN * NK + SPARE for g in GROUPS]


def z_shift(a, d):
    route = [(y * NZ + z, y * NZ + (z + d) % NZ) for y in range(NY) for z in range(NZ)]
    return lax.ppermute(a, "seq", route)


def y_shift(a, d):
    route = [(y * NZ + z, (y + d) % NY * NZ + z) for y in range(NY) for z in range(NZ)]
    return lax.ppermute(a, "seq", route)


def plan_kernel(me_ref, order_ref, smask_ref, vmask_ref, rate_ref, count_ref, *list_refs):
    me = me_ref[0]
    y, z = me // NZ, me % NZ
    for g, (group, out) in enumerate(zip(GROUPS, list_refs)):
        n = jnp.int32(0)
        for place, slot in enumerate(group):
            first = (y * NZ + (z - slot + NZ) % NZ) * OWN

            def row(i, n, place=place, first=first, out=out):
                bq = order_ref[first + i]
                for t in range(NY):
                    kfirst = ((y - t + NY) % NY * NZ + z) * OWN
                    for j in range(OWN):
                        bk = order_ref[kfirst + j]
                        live = jnp.where((smask_ref[bq, bk] > 0) & (bk <= bq), 1, 0)
                        diag = jnp.where(bk == bq, 1, 0)
                        out[n] = (place * OWN + i) + (t * OWN + j) * 64 + bq * 1024 + diag * 262144
                        n = n + live
                return n

            n = lax.fori_loop(0, OWN, row, n)
        for s in range(UNROLL):
            out[n + s] = jnp.int32(BLK * 1024)
        count_ref[g] = n
    ids_r = lax.broadcasted_iota(i32, (BLK, BLK), 0)
    ids_c = lax.broadcasted_iota(i32, (BLK, BLK), 1)
    mask = vmask_ref[...].astype(f32)
    below = jnp.sum(jnp.where(ids_c < ids_r, mask, 0.0), axis=1, keepdims=True)
    diag = jnp.sum(jnp.where(ids_c == ids_r, mask, 0.0), axis=1, keepdims=True)
    count = below * float(BLK) + diag * (ids_c + 1).astype(f32)
    rate_ref[pl.ds(0, BLK), :] = 1.0 / jnp.sqrt(jnp.maximum(count, 1.0))
    rate_ref[pl.ds(BLK, 8), :] = jnp.zeros((8, BLK), f32)


def make_plan(me, block_order, block_mask):
    smem = pl.BlockSpec(memory_space=pltpu.SMEM)
    vmem = pl.BlockSpec(memory_space=pltpu.VMEM)
    return pl.pallas_call(
        plan_kernel,
        out_shape=[
            jax.ShapeDtypeStruct((BLK + 8, BLK), f32),
            jax.ShapeDtypeStruct((len(GROUPS),), i32),
        ]
        + [jax.ShapeDtypeStruct((n,), i32) for n in list_sizes()],
        in_specs=[smem, smem, smem, vmem],
        out_specs=[vmem, smem] + [smem] * len(GROUPS),
        cost_estimate=pl.CostEstimate(flops=10_000, bytes_accessed=200_000, transcendentals=0),
    )(me, block_order, block_mask, block_mask)


def pairs_kernel(g, first, last, n_slots, *refs):
    refs = list(refs)
    take = lambda n: [refs.pop(0) for _ in range(n)]
    count_ref, list_ref, rate_ref = take(3)
    q_in, g_in = take(n_slots), take(n_slots)
    k_in, v_in = take(NY), take(NY)
    acc_in = [] if first else take(2)
    dq_out = take(n_slots)
    kv_out = take(NY + 1) if last else take(2)
    q_s, g_s, k_s, v_s, dq_s = take(5)
    dk_s, dv_s = take(2) if last else kv_out
    sem = take(1)[0]
    rows = OWN * BLK
    copies = []
    for ins, dst in ((q_in, q_s), (g_in, g_s), (k_in, k_s), (v_in, v_s)):
        for i, src in enumerate(ins):
            copies.append(
                pltpu.make_async_copy(src, dst.at[pl.ds(i * rows, rows), :], sem.at[len(copies)])
            )
    if not first:
        for src, dst in zip(acc_in, (dk_s, dv_s)):
            copies.append(pltpu.make_async_copy(src, dst, sem.at[len(copies)]))
    for c in copies:
        c.start()
    dq_s[...] = jnp.zeros_like(dq_s)
    if first:
        dk_s[...] = jnp.zeros_like(dk_s)
        dv_s[...] = jnp.zeros_like(dv_s)
    for c in copies:
        c.wait()
    scale = BLK ** (-0.5)
    masked = 0 in GROUPS[g]
    ahead = lax.broadcasted_iota(i32, (BLK, BLK), 1) - lax.broadcasted_iota(i32, (BLK, BLK), 0)
    across = (((1,), (1,)), ((), ()))
    down = (((0,), (0,)), ((), ()))

    def step(t, carry):
        entries = [list_ref[t * UNROLL + u] for u in range(UNROLL)]
        qs = [pl.ds(pl.multiple_of((e % 64) * BLK, BLK), BLK) for e in entries]
        ks = [pl.ds(pl.multiple_of((e // 64 % 16) * BLK, BLK), BLK) for e in entries]
        parts = []
        for e, q, k in zip(entries, qs, ks):
            rate = rate_ref[pl.ds(e // 1024 % 256, 1), :]
            s = lax.dot_general(k_s[k, :], q_s[q, :], across, preferred_element_type=f32) * scale
            sig = jax.nn.sigmoid(s)
            w = sig * rate
            if masked:
                w = jnp.where(ahead >= jnp.where(e >= 262144, 0, -BLK), w, 0.0)
            a = s * w
            da = lax.dot_general(v_s[k, :], g_s[q, :], across, preferred_element_type=f32)
            ds = (da * (w + a * (1.0 - sig))).astype(bf16)
            parts.append((a.astype(bf16), ds))
        sums = []
        for q, k, (a, ds) in zip(qs, ks, parts):
            dv = jnp.dot(a, g_s[q, :], preferred_element_type=f32)
            dk = jnp.dot(ds, q_s[q, :], preferred_element_type=f32)
            dq = lax.dot_general(ds, k_s[k, :], down, preferred_element_type=f32)
            sums.append((dq, dk, dv))
        for q, k, (dq, dk, dv) in zip(qs, ks, sums):
            dv_s[k, :] += dv
            dk_s[k, :] += dk
            dq_s[q, :] += dq
        return carry

    lax.fori_loop(0, (count_ref[g] + UNROLL - 1) // UNROLL, step, 0)
    for i, out in enumerate(dq_out):
        out[...] = dq_s[pl.ds(i * rows, rows), :].astype(out.dtype)
    if last:
        kv_out[0][pl.ds(0, rows), :] = dk_s[pl.ds(0, rows), :] * scale
        kv_out[1][pl.ds(0, rows), :] = dv_s[pl.ds(0, rows), :]
        for t in range(1, NY):
            kv_out[t + 1][pl.ds(0, rows), :] = dk_s[pl.ds(t * rows, rows), :].astype(bf16)
            kv_out[t + 1][pl.ds(rows, rows), :] = dv_s[pl.ds(t * rows, rows), :].astype(bf16)


def run_pairs(g, plan, q, gr, k, v, acc):
    rate, count, lists = plan[0], plan[1], plan[2:]
    first, last = g == 0, g == len(GROUPS) - 1
    n = len(GROUPS[g])
    rows = OWN * BLK
    smem = pl.BlockSpec(memory_space=pltpu.SMEM)
    vmem = pl.BlockSpec(memory_space=pltpu.VMEM)
    hbm = pl.BlockSpec(memory_space=pl.ANY)
    sds = jax.ShapeDtypeStruct
    outs = [sds((rows, BLK), f32 if s == 0 else bf16) for s in GROUPS[g]]
    if last:
        outs += [sds((rows, BLK), f32)] * 2 + [sds((2 * rows, BLK), bf16)] * (NY - 1)
    else:
        outs += [sds((NY * rows, BLK), f32)] * 2
    scratch = [
        pltpu.VMEM((n * rows, BLK), bf16),
        pltpu.VMEM((n * rows, BLK), bf16),
        pltpu.VMEM((NY * rows, BLK), bf16),
        pltpu.VMEM((NY * rows, BLK), bf16),
        pltpu.VMEM((n * rows, BLK), f32),
    ]
    if last:
        scratch += [pltpu.VMEM((NY * rows, BLK), f32)] * 2
    scratch.append(pltpu.SemaphoreType.DMA((2 * n + 2 * NY + 2,)))
    tiles = 4 * n
    return pl.pallas_call(
        functools.partial(pairs_kernel, g, first, last, n),
        out_shape=outs,
        in_specs=[smem, smem, vmem] + [hbm] * (2 * n + 2 * NY + len(acc)),
        out_specs=[vmem] * len(outs),
        scratch_shapes=scratch,
        compiler_params=pltpu.CompilerParams(vmem_limit_bytes=32 * 1024 * 1024),
        cost_estimate=pl.CostEstimate(
            flops=tiles * 10 * BLK**3, bytes_accessed=4_000_000, transcendentals=tiles * BLK * BLK
        ),
    )(count, lists[g], rate, *q, *gr, *k, *v, *acc)


def on_device(queries, keys, values, out_grad, block_mask, block_order):
    scale = BLK ** (-0.5)
    me = lax.axis_index("seq").astype(i32).reshape(1)
    plan = make_plan(me, block_order, block_mask)
    k = [keys] + [y_shift(keys, t) for t in range(1, NY)]
    v = [values] + [y_shift(values, t) for t in range(1, NY)]
    q, gr = {0: queries}, {0: out_grad}
    for s in range(1, NZ // 2):
        for part in (q, gr):
            part[s] = z_shift(part[s - 1], 1)
            part[NZ - s] = z_shift(part[(NZ - s + 1) % NZ], -1)
    half = NZ // 2
    q[half] = z_shift(q[half - 1], 1)
    gr[half] = z_shift(gr[half + 1], -1)

    back, acc = {}, ()
    for g, group in enumerate(GROUPS):
        out = run_pairs(g, plan, [q[s] for s in group], [gr[s] for s in group], k, v, acc)
        for s, dq in zip(group, out):
            back[s] = dq if s == 0 else z_shift(dq, -s)
        acc = tuple(out[len(group) :])
    own_k, own_v = acc[0], acc[1]
    kv_back = [y_shift(acc[t + 1], -t) for t in range(1, NY)]
    query_grad = sum(back[s].astype(f32) for s in range(NZ)) * scale
    rows = queries.shape[0]
    key_grad = own_k + sum(p[:rows].astype(f32) for p in kv_back) * scale
    value_grad = own_v + sum(p[rows:].astype(f32) for p in kv_back)
    return query_grad, key_grad, value_grad


def solution(mesh):
    whole = P(("rep", "seq"), "head")
    return jax.shard_map(
        on_device,
        mesh=mesh,
        in_specs=(whole, whole, whole, whole, P(), P()),
        out_specs=(whole, whole, whole),
        check_vma=False,
    )
```

```python
import functools

import jax
import jax.numpy as jnp
from jax import lax
from jax.experimental import pallas as pl
from jax.experimental.pallas import tpu as pltpu
from jax.sharding import PartitionSpec as P

BLK = 128
NZ = 8
NY = 4
OWN = 4
NK = NY * OWN
UNROLL = 8
SPARE = 8
GROUPS = ((0, 1, 7, 2, 6), (3, 5, 4))
bf16, f32, i32 = jnp.bfloat16, jnp.float32, jnp.int32


def list_sizes():
    return [len(g) * OWN * NK + SPARE for g in GROUPS]


def z_shift(a, d):
    route = [(y * NZ + z, y * NZ + (z + d) % NZ) for y in range(NY) for z in range(NZ)]
    return lax.ppermute(a, "seq", route)


def y_shift(a, d):
    route = [(y * NZ + z, (y + d) % NY * NZ + z) for y in range(NY) for z in range(NZ)]
    return lax.ppermute(a, "seq", route)


def plan_kernel(me_ref, order_ref, smask_ref, vmask_ref, rate_ref, count_ref, *list_refs):
    me = me_ref[0]
    y, z = me // NZ, me % NZ
    kfirsts = [((y - t + NY) % NY * NZ + z) * OWN for t in range(NY)]
    bks = [order_ref[kfirsts[t] + j] for t in range(NY) for j in range(OWN)]
    for g, (group, out) in enumerate(zip(GROUPS, list_refs)):
        n = jnp.int32(0)
        for place, slot in enumerate(group):
            first = (y * NZ + (z - slot + NZ) % NZ) * OWN

            def row(i, n, place=place, slot=slot, first=first, out=out):
                bq = order_ref[first + i]
                head = place * OWN + i + bq * 1024
                for c, bk in enumerate(bks):
                    live = (smask_ref[bq, bk] > 0) & (bk <= bq)
                    entry = head + c * 64
                    if slot == 0 and c < OWN:
                        entry = entry + jnp.where(bk == bq, 262144, 0)
                    out[n] = entry
                    n = n + jnp.where(live, 1, 0)
                return n

            n = lax.fori_loop(0, OWN, row, n)
        for s in range(UNROLL):
            out[n + s] = jnp.int32(BLK * 1024)
        count_ref[g] = n
    ids_r = lax.broadcasted_iota(i32, (BLK, BLK), 0)
    ids_c = lax.broadcasted_iota(i32, (BLK, BLK), 1)
    mask = vmask_ref[...].astype(f32)
    below = jnp.sum(jnp.where(ids_c < ids_r, mask, 0.0), axis=1, keepdims=True)
    diag = jnp.sum(jnp.where(ids_c == ids_r, mask, 0.0), axis=1, keepdims=True)
    count = below * float(BLK) + diag * (ids_c + 1).astype(f32)
    rate_ref[pl.ds(0, BLK), :] = 1.0 / jnp.sqrt(jnp.maximum(count, 1.0))
    rate_ref[pl.ds(BLK, 8), :] = jnp.zeros((8, BLK), f32)


def stack_kernel(a_ref, b_ref, ab_ref, sem):
    rows = a_ref.shape[0]
    copies = [
        pltpu.make_async_copy(src, ab_ref.at[pl.ds(i * rows, rows), :], sem.at[i])
        for i, src in enumerate((a_ref, b_ref))
    ]
    for c in copies:
        c.start()
    for c in copies:
        c.wait()


def stack_pair(a, b):
    return pl.pallas_call(
        stack_kernel,
        out_shape=jax.ShapeDtypeStruct((2 * a.shape[0], a.shape[1]), a.dtype),
        in_specs=[pl.BlockSpec(memory_space=pltpu.HBM)] * 2,
        out_specs=pl.BlockSpec(memory_space=pltpu.VMEM),
        scratch_shapes=[pltpu.SemaphoreType.DMA((2,))],
        cost_estimate=pl.CostEstimate(flops=0, bytes_accessed=500_000, transcendentals=0),
    )(a, b)


def make_plan(me, block_order, block_mask):
    smem = pl.BlockSpec(memory_space=pltpu.SMEM)
    vmem = pl.BlockSpec(memory_space=pltpu.VMEM)
    return pl.pallas_call(
        plan_kernel,
        out_shape=[
            jax.ShapeDtypeStruct((BLK + 8, BLK), f32),
            jax.ShapeDtypeStruct((len(GROUPS),), i32),
        ]
        + [jax.ShapeDtypeStruct((n,), i32) for n in list_sizes()],
        in_specs=[smem, smem, smem, vmem],
        out_specs=[vmem, smem] + [smem] * len(GROUPS),
        cost_estimate=pl.CostEstimate(flops=10_000, bytes_accessed=200_000, transcendentals=0),
    )(me, block_order, block_mask, block_mask)


def pairs_kernel(g, first, last, row_parts, *refs):
    refs = list(refs)
    take = lambda n: [refs.pop(0) for _ in range(n)]
    n_slots = len(GROUPS[g])
    count_ref, list_ref, rate_ref = take(3)
    row_in = take(len(row_parts))
    kv_in = take(NY)
    acc_in = [] if first else take(2)
    dq_out = take(n_slots)
    kv_out = take(NY + 1) if last else take(2)
    q_s, g_s, k_s, v_s, dq_s = take(5)
    dk_s, dv_s = take(2) if last else kv_out
    rows = OWN * BLK

    def fetch(src, at, dst, place):
        dst[pl.ds(place * rows, rows), :] = src[pl.ds(at, rows), :]

    for src, (place, kind) in zip(row_in, row_parts):
        if kind != "g":
            fetch(src, 0, q_s, place)
        if kind != "q":
            fetch(src, rows if kind == "qg" else 0, g_s, place)
    for t, src in enumerate(kv_in):
        fetch(src, 0, k_s, t)
        fetch(src, rows, v_s, t)
    dq_s[...] = jnp.zeros_like(dq_s)
    dk_s[...] = jnp.zeros_like(dk_s)
    dv_s[...] = jnp.zeros_like(dv_s)
    scale = BLK ** (-0.5)
    masked = 0 in GROUPS[g]
    ahead = lax.broadcasted_iota(i32, (BLK, BLK), 1) - lax.broadcasted_iota(i32, (BLK, BLK), 0)
    across = (((1,), (1,)), ((), ()))
    down = (((0,), (0,)), ((), ()))

    def step(t, carry):
        entries = [list_ref[t * UNROLL + u] for u in range(UNROLL)]
        qs = [pl.ds(pl.multiple_of((e % 64) * BLK, BLK), BLK) for e in entries]
        ks = [pl.ds(pl.multiple_of((e // 64 % 16) * BLK, BLK), BLK) for e in entries]
        parts = []
        for e, q, k in zip(entries, qs, ks):
            rate = rate_ref[pl.ds(e // 1024 % 256, 1), :]
            s = lax.dot_general(k_s[k, :], q_s[q, :], across, preferred_element_type=f32) * scale
            sig = jax.nn.sigmoid(s)
            w = sig * rate
            if masked:
                w = jnp.where(ahead >= jnp.where(e >= 262144, 0, -BLK), w, 0.0)
            a = s * w
            da = lax.dot_general(v_s[k, :], g_s[q, :], across, preferred_element_type=f32)
            ds = (da * (w + a * (1.0 - sig))).astype(bf16)
            parts.append((a.astype(bf16), ds))
        sums = []
        for q, k, (a, ds) in zip(qs, ks, parts):
            dv = jnp.dot(a, g_s[q, :], preferred_element_type=f32)
            dk = jnp.dot(ds, q_s[q, :], preferred_element_type=f32)
            dq = lax.dot_general(ds, k_s[k, :], down, preferred_element_type=f32)
            sums.append((dq, dk, dv))
        for q, k, (dq, dk, dv) in zip(qs, ks, sums):
            dv_s[k, :] += dv
            dk_s[k, :] += dk
            dq_s[q, :] += dq
        return carry

    lax.fori_loop(0, (count_ref[g] + UNROLL - 1) // UNROLL, step, 0)
    for i, out in enumerate(dq_out):
        out[...] = dq_s[pl.ds(i * rows, rows), :].astype(out.dtype)
    if last:
        for t in range(NY):
            own = pl.ds(t * rows, rows)
            dk, dv = [
                sum((p[own, :] for p in earlier), s[own, :])
                for s, earlier in ((dk_s, acc_in[:1]), (dv_s, acc_in[1:]))
            ]
            if t == 0:
                kv_out[0][...] = dk * scale
                kv_out[1][...] = dv
            else:
                kv_out[t + 1][pl.ds(0, rows), :] = dk.astype(bf16)
                kv_out[t + 1][pl.ds(rows, rows), :] = dv.astype(bf16)


def run_pairs(g, plan, row_shards, kv, acc):
    rate, count, lists = plan[0], plan[1], plan[2:]
    first, last = g == 0, g == len(GROUPS) - 1
    n = len(GROUPS[g])
    rows = OWN * BLK
    smem = pl.BlockSpec(memory_space=pltpu.SMEM)
    vmem = pl.BlockSpec(memory_space=pltpu.VMEM)
    sds = jax.ShapeDtypeStruct
    row_parts, row_arrays = [], []
    for place, s in enumerate(GROUPS[g]):
        for kind, array in row_shards[s].items():
            row_parts.append((place, kind))
            row_arrays.append(array)
    outs = [sds((rows, BLK), f32 if s == 0 else bf16) for s in GROUPS[g]]
    if last:
        outs += [sds((rows, BLK), f32)] * 2 + [sds((2 * rows, BLK), bf16)] * (NY - 1)
    else:
        outs += [sds((NY * rows, BLK), f32)] * 2
    scratch = [
        pltpu.VMEM((n * rows, BLK), bf16),
        pltpu.VMEM((n * rows, BLK), bf16),
        pltpu.VMEM((NY * rows, BLK), bf16),
        pltpu.VMEM((NY * rows, BLK), bf16),
        pltpu.VMEM((n * rows, BLK), f32),
    ]
    if last:
        scratch += [pltpu.VMEM((NY * rows, BLK), f32)] * 2
    tiles = 4 * n
    return pl.pallas_call(
        functools.partial(pairs_kernel, g, first, last, row_parts),
        out_shape=outs,
        in_specs=[smem, smem] + [vmem] * (1 + len(row_arrays) + NY + len(acc)),
        out_specs=[vmem] * len(outs),
        scratch_shapes=scratch,
        compiler_params=pltpu.CompilerParams(vmem_limit_bytes=32 * 1024 * 1024),
        cost_estimate=pl.CostEstimate(
            flops=tiles * 10 * BLK**3, bytes_accessed=4_000_000, transcendentals=tiles * BLK * BLK
        ),
    )(count, lists[g], rate, *row_arrays, *kv, *acc)


def on_device(queries, keys, values, out_grad, block_mask, block_order):
    scale = BLK ** (-0.5)
    rows = queries.shape[0]
    me = lax.axis_index("seq").astype(i32).reshape(1)
    plan = make_plan(me, block_order, block_mask)
    qg, kv = stack_pair(queries, out_grad), stack_pair(keys, values)
    ahead, behind = z_shift(qg, 1), z_shift(qg, -1)
    kvs = [kv] + [y_shift(kv, t) for t in (1, 3, 2)]
    kvs = [kvs[0], kvs[1], kvs[3], kvs[2]]
    (ahead, behind), plan = lax.optimization_barrier(((ahead, behind), plan))
    shards = {0: {"qg": qg}, 1: {"qg": ahead}, NZ - 1: {"qg": behind}}
    split = lambda a: {"q": a[:rows], "g": a[rows:]}
    ahead, behind = split(ahead), split(behind)
    for s in range(2, NZ // 2):
        ahead = {kind: z_shift(a, 1) for kind, a in ahead.items()}
        behind = {kind: z_shift(a, -1) for kind, a in behind.items()}
        shards[s], shards[NZ - s] = ahead, behind
    back, acc = {}, ()
    for g, group in enumerate(GROUPS):
        out = run_pairs(g, plan, shards, kvs, acc)
        if g == 0:
            ahead, behind, out = lax.optimization_barrier((ahead, behind, out))
            shards[NZ // 2 - 1], shards[NZ // 2 + 1] = ahead, behind
            shards[NZ // 2] = {"q": z_shift(ahead["q"], 1), "g": z_shift(behind["g"], -1)}
        acc = tuple(out[len(group) :])
        if g == len(GROUPS) - 1:
            kv_back = [y_shift(acc[t + 1], -t) for t in (2, 1, 3)]
        for s, dq in reversed(list(zip(group, out))):
            back[s] = dq if s == 0 else z_shift(dq, -s)
    own_k, own_v = acc[0], acc[1]
    query_grad = sum(back[s].astype(f32) for s in range(NZ)) * scale
    key_grad = own_k + sum(p[:rows].astype(f32) for p in kv_back) * scale
    value_grad = own_v + sum(p[rows:].astype(f32) for p in kv_back)
    return query_grad, key_grad, value_grad


def solution(mesh):
    whole = P(("rep", "seq"), "head")
    return jax.shard_map(
        on_device,
        mesh=mesh,
        in_specs=(whole, whole, whole, whole, P(), P()),
        out_specs=(whole, whole, whole),
        check_vma=False,
    )
```

```python
import functools

import jax
import jax.numpy as jnp
from jax import lax
from jax.experimental import pallas as pl
from jax.experimental.pallas import tpu as pltpu
from jax.sharding import PartitionSpec as P

BLK = 128
NZ = 8
NY = 4
OWN = 4
NK = NY * OWN
UNROLL = 8
SPARE = 8
GROUPS = ((0, 1, 7, 2, 6), (3, 5, 4))
bf16, f32, i32 = jnp.bfloat16, jnp.float32, jnp.int32


def list_sizes():
    return [len(g) * OWN * NK + SPARE for g in GROUPS]


def z_shift(a, d):
    route = [(y * NZ + z, y * NZ + (z + d) % NZ) for y in range(NY) for z in range(NZ)]
    return lax.ppermute(a, "seq", route)


def y_shift(a, d):
    route = [(y * NZ + z, (y + d) % NY * NZ + z) for y in range(NY) for z in range(NZ)]
    return lax.ppermute(a, "seq", route)


def plan_kernel(me_ref, order_ref, smask_ref, vmask_ref, rate_ref, count_ref, *list_refs):
    me = me_ref[0]
    y, z = me // NZ, me % NZ
    kfirsts = [((y - t + NY) % NY * NZ + z) * OWN for t in range(NY)]
    bks = [order_ref[kfirsts[t] + j] for t in range(NY) for j in range(OWN)]
    for g, (group, out) in enumerate(zip(GROUPS, list_refs)):
        n = jnp.int32(0)
        for place, slot in enumerate(group):
            first = (y * NZ + (z - slot + NZ) % NZ) * OWN

            def row(i, n, place=place, slot=slot, first=first, out=out):
                bq = order_ref[first + i]
                head = place * OWN + i + bq * 1024
                for c, bk in enumerate(bks):
                    live = (smask_ref[bq, bk] > 0) & (bk <= bq)
                    entry = head + c * 64
                    if slot == 0 and c < OWN:
                        entry = entry + jnp.where(bk == bq, 262144, 0)
                    out[n] = entry
                    n = n + jnp.where(live, 1, 0)
                return n

            n = lax.fori_loop(0, OWN, row, n)
        for s in range(UNROLL):
            out[n + s] = jnp.int32(BLK * 1024)
        count_ref[g] = n
    ids_r = lax.broadcasted_iota(i32, (BLK, BLK), 0)
    ids_c = lax.broadcasted_iota(i32, (BLK, BLK), 1)
    mask = vmask_ref[...].astype(f32)
    below = jnp.sum(jnp.where(ids_c < ids_r, mask, 0.0), axis=1, keepdims=True)
    diag = jnp.sum(jnp.where(ids_c == ids_r, mask, 0.0), axis=1, keepdims=True)
    count = below * float(BLK) + diag * (ids_c + 1).astype(f32)
    rate_ref[pl.ds(0, BLK), :] = 1.0 / jnp.sqrt(jnp.maximum(count, 1.0))
    rate_ref[pl.ds(BLK, 8), :] = jnp.zeros((8, BLK), f32)


def stack_kernel(a_ref, b_ref, c_ref, d_ref, ab_ref, cd_ref, sem):
    rows = a_ref.shape[0]
    copies = [
        pltpu.make_async_copy(src, dst.at[pl.ds(at, rows), :], sem.at[i])
        for i, (src, dst, at) in enumerate(
            ((a_ref, ab_ref, 0), (b_ref, ab_ref, rows), (c_ref, cd_ref, 0), (d_ref, cd_ref, rows))
        )
    ]
    for c in copies:
        c.start()
    for c in copies:
        c.wait()


def stack_pairs(a, b, c, d):
    out = jax.ShapeDtypeStruct((2 * a.shape[0], a.shape[1]), a.dtype)
    return pl.pallas_call(
        stack_kernel,
        out_shape=[out, out],
        in_specs=[pl.BlockSpec(memory_space=pltpu.HBM)] * 4,
        out_specs=[pl.BlockSpec(memory_space=pltpu.VMEM)] * 2,
        scratch_shapes=[pltpu.SemaphoreType.DMA((4,))],
        cost_estimate=pl.CostEstimate(flops=0, bytes_accessed=1_000_000, transcendentals=0),
    )(a, b, c, d)


def make_plan(me, block_order, block_mask):
    smem = pl.BlockSpec(memory_space=pltpu.SMEM)
    vmem = pl.BlockSpec(memory_space=pltpu.VMEM)
    return pl.pallas_call(
        plan_kernel,
        out_shape=[
            jax.ShapeDtypeStruct((BLK + 8, BLK), f32),
            jax.ShapeDtypeStruct((len(GROUPS),), i32),
        ]
        + [jax.ShapeDtypeStruct((n,), i32) for n in list_sizes()],
        in_specs=[smem, smem, smem, vmem],
        out_specs=[vmem, smem] + [smem] * len(GROUPS),
        cost_estimate=pl.CostEstimate(flops=10_000, bytes_accessed=200_000, transcendentals=0),
    )(me, block_order, block_mask, block_mask)


def pairs_kernel(g, first, last, row_parts, *refs):
    refs = list(refs)
    take = lambda n: [refs.pop(0) for _ in range(n)]
    n_slots = len(GROUPS[g])
    count_ref, list_ref, rate_ref = take(3)
    row_in = take(len(row_parts))
    kv_in = take(NY)
    acc_in = [] if first else take(2)
    dq_out = take(n_slots)
    kv_out = take(NY + 1) if last else take(2)
    q_s, g_s, k_s, v_s, dq_s = take(5)
    dk_s, dv_s = take(2) if last else kv_out
    rows = OWN * BLK

    def fetch(src, at, dst, place):
        dst[pl.ds(place * rows, rows), :] = src[pl.ds(at, rows), :]

    for src, (place, kind) in zip(row_in, row_parts):
        if kind != "g":
            fetch(src, 0, q_s, place)
        if kind != "q":
            fetch(src, rows if kind == "qg" else 0, g_s, place)
    for t, src in enumerate(kv_in):
        fetch(src, 0, k_s, t)
        fetch(src, rows, v_s, t)
    dq_s[...] = jnp.zeros_like(dq_s)
    dk_s[...] = jnp.zeros_like(dk_s)
    dv_s[...] = jnp.zeros_like(dv_s)
    scale = BLK ** (-0.5)
    masked = 0 in GROUPS[g]
    ahead = lax.broadcasted_iota(i32, (BLK, BLK), 1) - lax.broadcasted_iota(i32, (BLK, BLK), 0)
    across = (((1,), (1,)), ((), ()))
    down = (((0,), (0,)), ((), ()))

    def step(t, carry):
        entries = [list_ref[t * UNROLL + u] for u in range(UNROLL)]
        qs = [pl.ds(pl.multiple_of((e % 64) * BLK, BLK), BLK) for e in entries]
        ks = [pl.ds(pl.multiple_of((e // 64 % 16) * BLK, BLK), BLK) for e in entries]
        parts = []
        for e, q, k in zip(entries, qs, ks):
            rate = rate_ref[pl.ds(e // 1024 % 256, 1), :]
            s = lax.dot_general(k_s[k, :], q_s[q, :], across, preferred_element_type=f32) * scale
            sig = jax.nn.sigmoid(s)
            w = sig * rate
            if masked:
                w = jnp.where(ahead >= jnp.where(e >= 262144, 0, -BLK), w, 0.0)
            a = s * w
            da = lax.dot_general(v_s[k, :], g_s[q, :], across, preferred_element_type=f32)
            ds = (da * (w + a * (1.0 - sig))).astype(bf16)
            parts.append((a.astype(bf16), ds))
        sums = []
        for q, k, (a, ds) in zip(qs, ks, parts):
            dv = jnp.dot(a, g_s[q, :], preferred_element_type=f32)
            dk = jnp.dot(ds, q_s[q, :], preferred_element_type=f32)
            dq = lax.dot_general(ds, k_s[k, :], down, preferred_element_type=f32)
            sums.append((dq, dk, dv))
        for q, k, (dq, dk, dv) in zip(qs, ks, sums):
            dv_s[k, :] += dv
            dk_s[k, :] += dk
            dq_s[q, :] += dq
        return carry

    lax.fori_loop(0, (count_ref[g] + UNROLL - 1) // UNROLL, step, 0)
    for i, out in enumerate(dq_out):
        out[...] = dq_s[pl.ds(i * rows, rows), :].astype(out.dtype)
    if last:
        for t in range(NY):
            own = pl.ds(t * rows, rows)
            dk, dv = [
                sum((p[own, :] for p in earlier), s[own, :])
                for s, earlier in ((dk_s, acc_in[:1]), (dv_s, acc_in[1:]))
            ]
            if t == 0:
                kv_out[0][...] = dk * scale
                kv_out[1][...] = dv
            else:
                kv_out[t + 1][pl.ds(0, rows), :] = dk.astype(bf16)
                kv_out[t + 1][pl.ds(rows, rows), :] = dv.astype(bf16)


def run_pairs(g, plan, row_shards, kv, acc):
    rate, count, lists = plan[0], plan[1], plan[2:]
    first, last = g == 0, g == len(GROUPS) - 1
    n = len(GROUPS[g])
    rows = OWN * BLK
    smem = pl.BlockSpec(memory_space=pltpu.SMEM)
    vmem = pl.BlockSpec(memory_space=pltpu.VMEM)
    sds = jax.ShapeDtypeStruct
    row_parts, row_arrays = [], []
    for place, s in enumerate(GROUPS[g]):
        for kind, array in row_shards[s].items():
            row_parts.append((place, kind))
            row_arrays.append(array)
    outs = [sds((rows, BLK), f32 if s == 0 else bf16) for s in GROUPS[g]]
    if last:
        outs += [sds((rows, BLK), f32)] * 2 + [sds((2 * rows, BLK), bf16)] * (NY - 1)
    else:
        outs += [sds((NY * rows, BLK), f32)] * 2
    scratch = [
        pltpu.VMEM((n * rows, BLK), bf16),
        pltpu.VMEM((n * rows, BLK), bf16),
        pltpu.VMEM((NY * rows, BLK), bf16),
        pltpu.VMEM((NY * rows, BLK), bf16),
        pltpu.VMEM((n * rows, BLK), f32),
    ]
    if last:
        scratch += [pltpu.VMEM((NY * rows, BLK), f32)] * 2
    tiles = 4 * n
    return pl.pallas_call(
        functools.partial(pairs_kernel, g, first, last, row_parts),
        out_shape=outs,
        in_specs=[smem, smem] + [vmem] * (1 + len(row_arrays) + NY + len(acc)),
        out_specs=[vmem] * len(outs),
        scratch_shapes=scratch,
        compiler_params=pltpu.CompilerParams(vmem_limit_bytes=32 * 1024 * 1024),
        cost_estimate=pl.CostEstimate(
            flops=tiles * 10 * BLK**3, bytes_accessed=4_000_000, transcendentals=tiles * BLK * BLK
        ),
    )(count, lists[g], rate, *row_arrays, *kv, *acc)


def on_device(queries, keys, values, out_grad, block_mask, block_order):
    scale = BLK ** (-0.5)
    rows = queries.shape[0]
    me = lax.axis_index("seq").astype(i32).reshape(1)
    plan = make_plan(me, block_order, block_mask)
    qg, kv = stack_pairs(queries, out_grad, keys, values)
    ahead, behind = z_shift(qg, 1), z_shift(qg, -1)
    kvs = [kv, y_shift(kv, 1), None, y_shift(kv, 3)]
    (ahead, behind), plan, kv = lax.optimization_barrier(((ahead, behind), plan, kv))
    kvs[2] = y_shift(kv, 2)
    shards = {0: {"qg": qg}, 1: {"qg": ahead}, NZ - 1: {"qg": behind}}
    split = lambda a: {"q": a[:rows], "g": a[rows:]}
    ahead, behind = split(ahead), split(behind)
    for s in range(2, NZ // 2):
        ahead = {kind: z_shift(a, 1) for kind, a in ahead.items()}
        behind = {kind: z_shift(a, -1) for kind, a in behind.items()}
        shards[s], shards[NZ - s] = ahead, behind
    back, acc = {}, ()
    for g, group in enumerate(GROUPS):
        out = run_pairs(g, plan, shards, kvs, acc)
        if g == 0:
            ahead, behind, out = lax.optimization_barrier((ahead, behind, out))
            shards[NZ // 2 - 1], shards[NZ // 2 + 1] = ahead, behind
            shards[NZ // 2] = {"q": z_shift(ahead["q"], 1), "g": z_shift(behind["g"], -1)}
        acc = tuple(out[len(group) :])
        if g == len(GROUPS) - 1:
            kv_back = [y_shift(acc[t + 1], -t) for t in (2, 1, 3)]
        for s, dq in reversed(list(zip(group, out))):
            back[s] = dq if s == 0 else z_shift(dq, -s)
    own_k, own_v = acc[0], acc[1]
    query_grad = sum(back[s].astype(f32) for s in range(NZ)) * scale
    key_grad = own_k + sum(p[:rows].astype(f32) for p in kv_back) * scale
    value_grad = own_v + sum(p[rows:].astype(f32) for p in kv_back)
    return query_grad, key_grad, value_grad


def solution(mesh):
    whole = P(("rep", "seq"), "head")
    return jax.shard_map(
        on_device,
        mesh=mesh,
        in_specs=(whole, whole, whole, whole, P(), P()),
        out_specs=(whole, whole, whole),
        check_vma=False,
    )
```

```python
import functools

import jax
import jax.numpy as jnp
from jax import lax
from jax.experimental import pallas as pl
from jax.experimental.pallas import tpu as pltpu
from jax.sharding import PartitionSpec as P

BLK = 128
NZ = 8
NY = 4
OWN = 4
NK = NY * OWN
UNROLL = 8
SPARE = 8
GROUPS = ((0, 1, 7, 2, 6), (3, 5, 4))
bf16, f32, i32 = jnp.bfloat16, jnp.float32, jnp.int32


def list_sizes():
    return [len(g) * OWN * NK + SPARE for g in GROUPS]


def z_shift(a, d):
    route = [(y * NZ + z, y * NZ + (z + d) % NZ) for y in range(NY) for z in range(NZ)]
    return lax.ppermute(a, "seq", route)


def y_shift(a, d):
    route = [(y * NZ + z, (y + d) % NY * NZ + z) for y in range(NY) for z in range(NZ)]
    return lax.ppermute(a, "seq", route)


def plan_kernel(me_ref, order_ref, smask_ref, vmask_ref, rate_ref, count_ref, *list_refs):
    me = me_ref[0]
    y, z = me // NZ, me % NZ
    kfirsts = [((y - t + NY) % NY * NZ + z) * OWN for t in range(NY)]
    bks = [order_ref[kfirsts[t] + j] for t in range(NY) for j in range(OWN)]
    for g, (group, out) in enumerate(zip(GROUPS, list_refs)):
        n = jnp.int32(0)
        for place, slot in enumerate(group):
            first = (y * NZ + (z - slot + NZ) % NZ) * OWN

            def row(i, n, place=place, slot=slot, first=first, out=out):
                bq = order_ref[first + i]
                head = place * OWN + i + bq * 1024
                for c, bk in enumerate(bks):
                    live = (smask_ref[bq, bk] > 0) & (bk <= bq)
                    entry = head + c * 64
                    if slot == 0 and c < OWN:
                        entry = entry + jnp.where(bk == bq, 262144, 0)
                    out[n] = entry
                    n = n + jnp.where(live, 1, 0)
                return n

            n = lax.fori_loop(0, OWN, row, n)
        for s in range(UNROLL):
            out[n + s] = jnp.int32(BLK * 1024)
        count_ref[g] = n
    ids_r = lax.broadcasted_iota(i32, (BLK, BLK), 0)
    ids_c = lax.broadcasted_iota(i32, (BLK, BLK), 1)
    mask = vmask_ref[...].astype(f32)
    below = jnp.sum(jnp.where(ids_c < ids_r, mask, 0.0), axis=1, keepdims=True)
    diag = jnp.sum(jnp.where(ids_c == ids_r, mask, 0.0), axis=1, keepdims=True)
    count = below * float(BLK) + diag * (ids_c + 1).astype(f32)
    rate_ref[pl.ds(0, BLK), :] = 1.0 / jnp.sqrt(jnp.maximum(count, 1.0))
    rate_ref[pl.ds(BLK, 8), :] = jnp.zeros((8, BLK), f32)


def stack_kernel(a_ref, b_ref, c_ref, d_ref, ab_ref, cd_ref, sem):
    rows = a_ref.shape[0]
    copies = [
        pltpu.make_async_copy(src, dst.at[pl.ds(at, rows), :], sem.at[i])
        for i, (src, dst, at) in enumerate(
            ((a_ref, ab_ref, 0), (b_ref, ab_ref, rows), (c_ref, cd_ref, 0), (d_ref, cd_ref, rows))
        )
    ]
    for c in copies:
        c.start()
    for c in copies:
        c.wait()


def stack_pairs(a, b, c, d):
    out = pltpu.VMEM((2 * a.shape[0], a.shape[1]), a.dtype)
    return pl.pallas_call(
        stack_kernel,
        out_shape=[out, out],
        in_specs=[pl.BlockSpec(memory_space=pltpu.HBM)] * 4,
        out_specs=[pl.BlockSpec(memory_space=pltpu.VMEM)] * 2,
        scratch_shapes=[pltpu.SemaphoreType.DMA((4,))],
        cost_estimate=pl.CostEstimate(flops=0, bytes_accessed=1_000_000, transcendentals=0),
    )(a, b, c, d)


def pack_kernel(ahead_ref, behind_ref, up_ref, down_ref, ahead_out, behind_out):
    rows = up_ref.shape[0]
    ahead_out[pl.ds(0, rows), :] = ahead_ref[pl.ds(0, rows), :]
    ahead_out[pl.ds(rows, rows), :] = up_ref[...]
    behind_out[pl.ds(0, rows), :] = behind_ref[pl.ds(rows, rows), :]
    behind_out[pl.ds(rows, rows), :] = down_ref[...]


def pack_last_step(ahead, behind, up, down):
    vmem = pl.BlockSpec(memory_space=pltpu.VMEM)
    return pl.pallas_call(
        pack_kernel,
        out_shape=[pltpu.VMEM(ahead.shape, ahead.dtype)] * 2,
        in_specs=[vmem] * 4,
        out_specs=[vmem] * 2,
        compiler_params=pltpu.CompilerParams(vmem_limit_bytes=2 * 1024 * 1024),
        cost_estimate=pl.CostEstimate(flops=0, bytes_accessed=500_000, transcendentals=0),
    )(ahead, behind, up, down)


def make_plan(me, block_order, block_mask):
    smem = pl.BlockSpec(memory_space=pltpu.SMEM)
    vmem = pl.BlockSpec(memory_space=pltpu.VMEM)
    return pl.pallas_call(
        plan_kernel,
        out_shape=[
            pltpu.VMEM((BLK + 8, BLK), f32),
            jax.ShapeDtypeStruct((len(GROUPS),), i32),
        ]
        + [jax.ShapeDtypeStruct((n,), i32) for n in list_sizes()],
        in_specs=[smem, smem, smem, vmem],
        out_specs=[vmem, smem] + [smem] * len(GROUPS),
        cost_estimate=pl.CostEstimate(flops=10_000, bytes_accessed=200_000, transcendentals=0),
    )(me, block_order, block_mask, block_mask)


def pairs_kernel(g, first, last, row_parts, *refs):
    refs = list(refs)
    take = lambda n: [refs.pop(0) for _ in range(n)]
    n_slots = len(GROUPS[g])
    count_ref, list_ref, rate_ref = take(3)
    row_in = take(len(row_parts))
    kv_in = take(NY)
    acc_in = [] if first else take(2)
    dq_out = take(n_slots)
    kv_out = take(NY + 1) if last else take(2)
    q_s, g_s, k_s, v_s, dq_s = take(5)
    dk_s, dv_s = take(2) if last else kv_out
    rows = OWN * BLK

    def fetch(src, at, dst, place):
        dst[pl.ds(place * rows, rows), :] = src[pl.ds(at, rows), :]

    for src, (place, kind) in zip(row_in, row_parts):
        if kind != "g":
            fetch(src, 0, q_s, place)
        if kind != "q":
            fetch(src, rows if kind == "qg" else 0, g_s, place)
    for t, src in enumerate(kv_in):
        fetch(src, 0, k_s, t)
        fetch(src, rows, v_s, t)
    dq_s[...] = jnp.zeros_like(dq_s)
    dk_s[...] = jnp.zeros_like(dk_s)
    dv_s[...] = jnp.zeros_like(dv_s)
    scale = BLK ** (-0.5)
    masked = 0 in GROUPS[g]
    ahead = lax.broadcasted_iota(i32, (BLK, BLK), 1) - lax.broadcasted_iota(i32, (BLK, BLK), 0)
    across = (((1,), (1,)), ((), ()))
    down = (((0,), (0,)), ((), ()))

    def step(t, carry):
        entries = [list_ref[t * UNROLL + u] for u in range(UNROLL)]
        qs = [pl.ds(pl.multiple_of((e % 64) * BLK, BLK), BLK) for e in entries]
        ks = [pl.ds(pl.multiple_of((e // 64 % 16) * BLK, BLK), BLK) for e in entries]
        parts = []
        for e, q, k in zip(entries, qs, ks):
            rate = rate_ref[pl.ds(e // 1024 % 256, 1), :]
            s = lax.dot_general(k_s[k, :], q_s[q, :], across, preferred_element_type=f32) * scale
            sig = jax.nn.sigmoid(s)
            w = sig * rate
            if masked:
                w = jnp.where(ahead >= jnp.where(e >= 262144, 0, -BLK), w, 0.0)
            a = s * w
            da = lax.dot_general(v_s[k, :], g_s[q, :], across, preferred_element_type=f32)
            ds = (da * (w + a * (1.0 - sig))).astype(bf16)
            parts.append((a.astype(bf16), ds))
        sums = []
        for q, k, (a, ds) in zip(qs, ks, parts):
            dv = jnp.dot(a, g_s[q, :], preferred_element_type=f32)
            dk = jnp.dot(ds, q_s[q, :], preferred_element_type=f32)
            dq = lax.dot_general(ds, k_s[k, :], down, preferred_element_type=f32)
            sums.append((dq, dk, dv))
        for q, k, (dq, dk, dv) in zip(qs, ks, sums):
            dv_s[k, :] += dv
            dk_s[k, :] += dk
            dq_s[q, :] += dq
        return carry

    lax.fori_loop(0, (count_ref[g] + UNROLL - 1) // UNROLL, step, 0)
    for i, out in enumerate(dq_out):
        out[...] = dq_s[pl.ds(i * rows, rows), :].astype(out.dtype)
    if last:
        for t in range(NY):
            own = pl.ds(t * rows, rows)
            dk, dv = [
                sum((p[own, :] for p in earlier), s[own, :])
                for s, earlier in ((dk_s, acc_in[:1]), (dv_s, acc_in[1:]))
            ]
            if t == 0:
                kv_out[0][...] = dk * scale
                kv_out[1][...] = dv
            else:
                kv_out[t + 1][pl.ds(0, rows), :] = dk.astype(bf16)
                kv_out[t + 1][pl.ds(rows, rows), :] = dv.astype(bf16)


def run_pairs(g, plan, row_shards, kv, acc):
    rate, count, lists = plan[0], plan[1], plan[2:]
    first, last = g == 0, g == len(GROUPS) - 1
    n = len(GROUPS[g])
    rows = OWN * BLK
    smem = pl.BlockSpec(memory_space=pltpu.SMEM)
    vmem = pl.BlockSpec(memory_space=pltpu.VMEM)
    sds = jax.ShapeDtypeStruct
    row_parts, row_arrays = [], []
    for place, s in enumerate(GROUPS[g]):
        for kind, array in row_shards[s].items():
            row_parts.append((place, kind))
            row_arrays.append(array)
    outs = [sds((rows, BLK), f32 if s == 0 else bf16) for s in GROUPS[g]]
    if last:
        outs += [sds((rows, BLK), f32)] * 2 + [sds((2 * rows, BLK), bf16)] * (NY - 1)
    else:
        outs += [sds((NY * rows, BLK), f32)] * 2
    scratch = [
        pltpu.VMEM((n * rows, BLK), bf16),
        pltpu.VMEM((n * rows, BLK), bf16),
        pltpu.VMEM((NY * rows, BLK), bf16),
        pltpu.VMEM((NY * rows, BLK), bf16),
        pltpu.VMEM((n * rows, BLK), f32),
    ]
    if last:
        scratch += [pltpu.VMEM((NY * rows, BLK), f32)] * 2
    tiles = 4 * n
    return pl.pallas_call(
        functools.partial(pairs_kernel, g, first, last, row_parts),
        out_shape=outs,
        in_specs=[smem, smem] + [vmem] * (1 + len(row_arrays) + NY + len(acc)),
        out_specs=[vmem] * len(outs),
        scratch_shapes=scratch,
        compiler_params=pltpu.CompilerParams(vmem_limit_bytes=16 * 1024 * 1024),
        cost_estimate=pl.CostEstimate(
            flops=tiles * 10 * BLK**3, bytes_accessed=4_000_000, transcendentals=tiles * BLK * BLK
        ),
    )(count, lists[g], rate, *row_arrays, *kv, *acc)


def on_device(queries, keys, values, out_grad, block_mask, block_order):
    scale = BLK ** (-0.5)
    rows = queries.shape[0]
    me = lax.axis_index("seq").astype(i32).reshape(1)
    plan = make_plan(me, block_order, block_mask)
    qg, kv = stack_pairs(queries, out_grad, keys, values)
    ahead, behind = z_shift(qg, 1), z_shift(qg, -1)
    far_kv = y_shift(kv, 2)
    (ahead, behind), plan, far_kv, kv = lax.optimization_barrier(
        ((ahead, behind), plan, far_kv, kv)
    )
    kvs = [kv, y_shift(kv, 1), far_kv, y_shift(kv, 3)]
    shards = {0: {"qg": qg}, 1: {"qg": ahead}, NZ - 1: {"qg": behind}}
    for s in range(2, NZ // 2):
        ahead, behind = z_shift(ahead, 1), z_shift(behind, -1)
        shards[s], shards[NZ - s] = {"qg": ahead}, {"qg": behind}

    back, acc = {}, ()
    for g, group in enumerate(GROUPS):
        out = run_pairs(g, plan, shards, kvs, acc)
        if g == 0:
            ahead, behind, out = lax.optimization_barrier((ahead, behind, out))
            shards[NZ // 2 - 1], shards[NZ // 2 + 1] = {"qg": ahead}, {"qg": behind}
            up, down = pack_last_step(
                ahead, behind, out[group.index(NZ - 1)], out[group.index(1)]
            )
            up, down = z_shift(up, 1), z_shift(down, -1)
            shards[NZ // 2] = {"q": up, "g": down}
            back[NZ - 1], back[1] = up[rows:], down[rows:]
        acc = tuple(out[len(group) :])
        if g == len(GROUPS) - 1:
            kv_back = [y_shift(acc[t + 1], -t) for t in (2, 1, 3)]
        for s, dq in reversed(list(zip(group, out))):
            if s not in back:
                back[s] = dq if s == 0 else z_shift(dq, -s)
    own_k, own_v = acc[0], acc[1]
    query_grad = sum(back[s].astype(f32) for s in range(NZ)) * scale
    key_grad = own_k + sum(p[:rows].astype(f32) for p in kv_back) * scale
    value_grad = own_v + sum(p[rows:].astype(f32) for p in kv_back)
    return query_grad, key_grad, value_grad


def solution(mesh):
    whole = P(("rep", "seq"), "head")
    return jax.shard_map(
        on_device,
        mesh=mesh,
        in_specs=(whole, whole, whole, whole, P(), P()),
        out_specs=(whole, whole, whole),
        check_vma=False,
    )
```

```python
import functools

import jax
import jax.numpy as jnp
from jax import lax
from jax.experimental import pallas as pl
from jax.experimental.pallas import tpu as pltpu
from jax.sharding import PartitionSpec as P

BLK = 128
NZ = 8
NY = 4
OWN = 4
NK = NY * OWN
UNROLL = 8
SPARE = 8
GROUPS = ((0, 1, 7, 2, 6), (3, 5, 4))
bf16, f32, i32 = jnp.bfloat16, jnp.float32, jnp.int32


def list_sizes():
    return [len(g) * OWN * NK + SPARE for g in GROUPS]


def z_shift(a, d):
    route = [(y * NZ + z, y * NZ + (z + d) % NZ) for y in range(NY) for z in range(NZ)]
    return lax.ppermute(a, "seq", route)


def y_shift(a, d):
    route = [(y * NZ + z, (y + d) % NY * NZ + z) for y in range(NY) for z in range(NZ)]
    return lax.ppermute(a, "seq", route)


def plan_kernel(me_ref, order_ref, smask_ref, vmask_ref, rate_ref, count_ref, *list_refs):
    me = me_ref[0]
    y, z = me // NZ, me % NZ
    kfirsts = [((y - t + NY) % NY * NZ + z) * OWN for t in range(NY)]
    bks = [order_ref[kfirsts[t] + j] for t in range(NY) for j in range(OWN)]
    for g, (group, out) in enumerate(zip(GROUPS, list_refs)):
        n = jnp.int32(0)
        for place, slot in enumerate(group):
            first = (y * NZ + (z - slot + NZ) % NZ) * OWN

            def row(i, n, place=place, slot=slot, first=first, out=out):
                bq = order_ref[first + i]
                head = place * OWN + i + bq * 1024
                for c, bk in enumerate(bks):
                    live = (smask_ref[bq, bk] > 0) & (bk <= bq)
                    entry = head + c * 64
                    if slot == 0 and c < OWN:
                        entry = entry + jnp.where(bk == bq, 262144, 0)
                    out[n] = entry
                    n = n + jnp.where(live, 1, 0)
                return n

            n = lax.fori_loop(0, OWN, row, n)
        for s in range(UNROLL):
            out[n + s] = jnp.int32(BLK * 1024)
        count_ref[g] = n
    ids_r = lax.broadcasted_iota(i32, (BLK, BLK), 0)
    ids_c = lax.broadcasted_iota(i32, (BLK, BLK), 1)
    mask = vmask_ref[...].astype(f32)
    below = jnp.sum(jnp.where(ids_c < ids_r, mask, 0.0), axis=1, keepdims=True)
    diag = jnp.sum(jnp.where(ids_c == ids_r, mask, 0.0), axis=1, keepdims=True)
    count = below * float(BLK) + diag * (ids_c + 1).astype(f32)
    rate_ref[pl.ds(0, BLK), :] = 1.0 / jnp.sqrt(jnp.maximum(count, 1.0))
    rate_ref[pl.ds(BLK, 8), :] = jnp.zeros((8, BLK), f32)


def stack_kernel(a_ref, b_ref, c_ref, d_ref, ab_ref, cd_ref, sem):
    rows = a_ref.shape[0]
    copies = [
        pltpu.make_async_copy(src, dst.at[pl.ds(at, rows), :], sem.at[i])
        for i, (src, dst, at) in enumerate(
            ((a_ref, ab_ref, 0), (b_ref, ab_ref, rows), (c_ref, cd_ref, 0), (d_ref, cd_ref, rows))
        )
    ]
    for c in copies:
        c.start()
    for c in copies:
        c.wait()


def stack_pairs(a, b, c, d):
    out = pltpu.VMEM((2 * a.shape[0], a.shape[1]), a.dtype)
    return pl.pallas_call(
        stack_kernel,
        out_shape=[out, out],
        in_specs=[pl.BlockSpec(memory_space=pltpu.HBM)] * 4,
        out_specs=[pl.BlockSpec(memory_space=pltpu.VMEM)] * 2,
        scratch_shapes=[pltpu.SemaphoreType.DMA((4,))],
        cost_estimate=pl.CostEstimate(flops=0, bytes_accessed=1_000_000, transcendentals=0),
    )(a, b, c, d)


def pack_kernel(ahead_ref, behind_ref, up_ref, down_ref, ahead_out, behind_out):
    rows = up_ref.shape[0]
    ahead_out[pl.ds(0, rows), :] = ahead_ref[pl.ds(0, rows), :]
    ahead_out[pl.ds(rows, rows), :] = up_ref[...]
    behind_out[pl.ds(0, rows), :] = behind_ref[pl.ds(rows, rows), :]
    behind_out[pl.ds(rows, rows), :] = down_ref[...]


def pack_last_step(ahead, behind, up, down):
    vmem = pl.BlockSpec(memory_space=pltpu.VMEM)
    return pl.pallas_call(
        pack_kernel,
        out_shape=[pltpu.VMEM(ahead.shape, ahead.dtype)] * 2,
        in_specs=[vmem] * 4,
        out_specs=[vmem] * 2,
        compiler_params=pltpu.CompilerParams(vmem_limit_bytes=2 * 1024 * 1024),
        cost_estimate=pl.CostEstimate(flops=0, bytes_accessed=500_000, transcendentals=0),
    )(ahead, behind, up, down)


def make_plan(me, block_order, block_mask):
    smem = pl.BlockSpec(memory_space=pltpu.SMEM)
    vmem = pl.BlockSpec(memory_space=pltpu.VMEM)
    return pl.pallas_call(
        plan_kernel,
        out_shape=[
            pltpu.VMEM((BLK + 8, BLK), f32),
            jax.ShapeDtypeStruct((len(GROUPS),), i32),
        ]
        + [jax.ShapeDtypeStruct((n,), i32) for n in list_sizes()],
        in_specs=[smem, smem, smem, vmem],
        out_specs=[vmem, smem] + [smem] * len(GROUPS),
        cost_estimate=pl.CostEstimate(flops=10_000, bytes_accessed=200_000, transcendentals=0),
    )(me, block_order, block_mask, block_mask)


def pairs_kernel(g, first, last, row_parts, *refs):
    refs = list(refs)
    take = lambda n: [refs.pop(0) for _ in range(n)]
    n_slots = len(GROUPS[g])
    count_ref, list_ref, rate_ref = take(3)
    row_in = take(len(row_parts))
    kv_in = take(NY)
    acc_in = [] if first else take(2)
    dq_out = take(n_slots)
    kv_out = take(NY + 1) if last else take(2)
    q_s, g_s, k_s, v_s, dq_s = take(5)
    dk_s, dv_s = take(2) if last else kv_out
    rows = OWN * BLK

    def fetch(src, at, dst, place):
        dst[pl.ds(place * rows, rows), :] = src[pl.ds(at, rows), :]

    for src, (place, kind) in zip(row_in, row_parts):
        if kind != "g":
            fetch(src, 0, q_s, place)
        if kind != "q":
            fetch(src, rows if kind == "qg" else 0, g_s, place)
    for t, src in enumerate(kv_in):
        fetch(src, 0, k_s, t)
        fetch(src, rows, v_s, t)
    dq_s[...] = jnp.zeros_like(dq_s)
    dk_s[...] = jnp.zeros_like(dk_s)
    dv_s[...] = jnp.zeros_like(dv_s)
    scale = BLK ** (-0.5)
    masked = 0 in GROUPS[g]
    ahead = lax.broadcasted_iota(i32, (BLK, BLK), 1) - lax.broadcasted_iota(i32, (BLK, BLK), 0)
    across = (((1,), (1,)), ((), ()))
    down = (((0,), (0,)), ((), ()))

    def step(t, carry):
        entries = [list_ref[t * UNROLL + u] for u in range(UNROLL)]
        qs = [pl.ds(pl.multiple_of((e % 64) * BLK, BLK), BLK) for e in entries]
        ks = [pl.ds(pl.multiple_of((e // 64 % 16) * BLK, BLK), BLK) for e in entries]
        parts = []
        for e, q, k in zip(entries, qs, ks):
            rate = rate_ref[pl.ds(e // 1024 % 256, 1), :]
            s = lax.dot_general(k_s[k, :], q_s[q, :], across, preferred_element_type=f32) * scale
            sig = jax.nn.sigmoid(s)
            w = sig * rate
            if masked:
                w = jnp.where(ahead >= jnp.where(e >= 262144, 0, -BLK), w, 0.0)
            a = s * w
            da = lax.dot_general(v_s[k, :], g_s[q, :], across, preferred_element_type=f32)
            ds = (da * (w + a * (1.0 - sig))).astype(bf16)
            parts.append((a.astype(bf16), ds))
        sums = []
        for q, k, (a, ds) in zip(qs, ks, parts):
            dv = jnp.dot(a, g_s[q, :], preferred_element_type=f32)
            dk = jnp.dot(ds, q_s[q, :], preferred_element_type=f32)
            dq = lax.dot_general(ds, k_s[k, :], down, preferred_element_type=f32)
            sums.append((dq, dk, dv))
        for q, k, (dq, dk, dv) in zip(qs, ks, sums):
            dv_s[k, :] += dv
            dk_s[k, :] += dk
            dq_s[q, :] += dq
        return carry

    lax.fori_loop(0, (count_ref[g] + UNROLL - 1) // UNROLL, step, 0)
    for i, out in enumerate(dq_out):
        out[...] = dq_s[pl.ds(i * rows, rows), :].astype(out.dtype)
    if last:
        for t in range(NY):
            own = pl.ds(t * rows, rows)
            dk, dv = [
                sum((p[own, :] for p in earlier), s[own, :])
                for s, earlier in ((dk_s, acc_in[:1]), (dv_s, acc_in[1:]))
            ]
            if t == 0:
                kv_out[0][...] = dk * scale
                kv_out[1][...] = dv
            else:
                kv_out[t + 1][pl.ds(0, rows), :] = dk.astype(bf16)
                kv_out[t + 1][pl.ds(rows, rows), :] = dv.astype(bf16)


def run_pairs(g, plan, row_shards, kv, acc):
    rate, count, lists = plan[0], plan[1], plan[2:]
    first, last = g == 0, g == len(GROUPS) - 1
    n = len(GROUPS[g])
    rows = OWN * BLK
    smem = pl.BlockSpec(memory_space=pltpu.SMEM)
    vmem = pl.BlockSpec(memory_space=pltpu.VMEM)
    sds = jax.ShapeDtypeStruct
    row_parts, row_arrays = [], []
    for place, s in enumerate(GROUPS[g]):
        for kind, array in row_shards[s].items():
            row_parts.append((place, kind))
            row_arrays.append(array)
    outs = [sds((rows, BLK), f32 if s == 0 else bf16) for s in GROUPS[g]]
    if last:
        outs += [sds((rows, BLK), f32)] * 2 + [sds((2 * rows, BLK), bf16)] * (NY - 1)
    else:
        outs += [sds((NY * rows, BLK), f32)] * 2
    scratch = [
        pltpu.VMEM((n * rows, BLK), bf16),
        pltpu.VMEM((n * rows, BLK), bf16),
        pltpu.VMEM((NY * rows, BLK), bf16),
        pltpu.VMEM((NY * rows, BLK), bf16),
        pltpu.VMEM((n * rows, BLK), f32),
    ]
    if last:
        scratch += [pltpu.VMEM((NY * rows, BLK), f32)] * 2
    tiles = 4 * n
    return pl.pallas_call(
        functools.partial(pairs_kernel, g, first, last, row_parts),
        out_shape=outs,
        in_specs=[smem, smem] + [vmem] * (1 + len(row_arrays) + NY + len(acc)),
        out_specs=[vmem] * len(outs),
        scratch_shapes=scratch,
        compiler_params=pltpu.CompilerParams(vmem_limit_bytes=16 * 1024 * 1024),
        cost_estimate=pl.CostEstimate(
            flops=tiles * 10 * BLK**3, bytes_accessed=4_000_000, transcendentals=tiles * BLK * BLK
        ),
    )(count, lists[g], rate, *row_arrays, *kv, *acc)


def on_device(queries, keys, values, out_grad, block_mask, block_order):
    scale = BLK ** (-0.5)
    rows = queries.shape[0]
    me = lax.axis_index("seq").astype(i32).reshape(1)
    plan = make_plan(me, block_order, block_mask)
    qg, kv = stack_pairs(queries, out_grad, keys, values)
    ahead, behind = z_shift(qg, 1), z_shift(qg, -1)
    far_kv = y_shift(kv, 2)
    (ahead, behind), plan, far_kv, kv = lax.optimization_barrier(
        ((ahead, behind), plan, far_kv, kv)
    )
    kvs = [kv, y_shift(kv, 1), far_kv, y_shift(kv, 3)]
    shards = {0: {"qg": qg}, 1: {"qg": ahead}, NZ - 1: {"qg": behind}}
    for s in range(2, NZ // 2):
        ahead, behind = z_shift(ahead, 1), z_shift(behind, -1)
        shards[s], shards[NZ - s] = {"qg": ahead}, {"qg": behind}

    back, acc = {}, ()
    for g, group in enumerate(GROUPS):
        out = run_pairs(g, plan, shards, kvs, acc)
        if g == 0:
            ahead, behind, out = lax.optimization_barrier((ahead, behind, out))
            shards[NZ // 2 - 1], shards[NZ // 2 + 1] = {"qg": ahead}, {"qg": behind}
            up, down = pack_last_step(
                ahead, behind, out[group.index(NZ - 1)], out[group.index(1)]
            )
            up, down = z_shift(up, 1), z_shift(down, -1)
            shards[NZ // 2] = {"q": up, "g": down}
            back[NZ - 1], back[1] = up[rows:], down[rows:]
        acc = tuple(out[len(group) :])
        if g == len(GROUPS) - 1:
            kv_back = [y_shift(acc[t + 1], -t) for t in (2, 1, 3)]
        for s, dq in reversed(list(zip(group, out))):
            if s not in back:
                back[s] = dq if s == 0 else z_shift(dq, -s)
    own_k, own_v = acc[0], acc[1]
    query_grad = sum(back[s].astype(f32) for s in range(NZ)) * scale
    early = (
        own_k + sum(p[:rows].astype(f32) for p in kv_back[:-1]) * scale,
        own_v + sum(p[rows:].astype(f32) for p in kv_back[:-1]),
    )
    early_k, early_v = lax.optimization_barrier(early)
    key_grad = early_k + kv_back[-1][:rows].astype(f32) * scale
    value_grad = early_v + kv_back[-1][rows:].astype(f32)
    return query_grad, key_grad, value_grad


def solution(mesh):
    whole = P(("rep", "seq"), "head")
    return jax.shard_map(
        on_device,
        mesh=mesh,
        in_specs=(whole, whole, whole, whole, P(), P()),
        out_specs=(whole, whole, whole),
        check_vma=False,
    )
```
